256 devices in a mesh: row: 16 (over y, z_hi, core), col: 16 (over x, z_lo).
Axes of the slice: x: 4, y: 4, z: 8 (z_hi: 2, z_lo: 4; z = z_hi * 4 + z_lo), core: 2. Of those that a mesh axis runs over, the one named last changes fastest.
Arguments:
- features: bfloat16 [131072, 128], P(('col', 'row')), may hold values from -6 to 6
- weight: bfloat16 [128, 256], replicated, may hold values from -0.5 to 0.5
- cotangent: bfloat16 [131072, 256], P(('row', 'col')), may hold values from -6 to 6
- adj_blocks: bfloat16 [16, 16, 256, 128, 128], P('row', 'col'), may hold values from -0.0625 to 0.0625
- block_rows: int32 [16, 16, 256], P('row', 'col'), may hold values from 0 to 63, as said below
- block_cols: int32 [16, 16, 256], P('row', 'col'), may hold values from 0 to 63, as said below
- live_mask: int32 [16, 16, 256], P('row', 'col'), may hold values from 0 to 1, as said below
Outputs:
- activated: bfloat16 [131072, 256], P(('row', 'col'))
- grad_input: bfloat16 [131072, 128], P(('col', 'row'))
- grad_weight: float32 [128, 256], replicated
The draws below stay inside these ranges and needn't reach their ends.
Inputs may be any that keep to these rules, and one draw needn't show every extreme that they name: `block_rows`: within one tile the 256 slots name distinct blocks. `block_cols`: together with block_rows, distinct blocks within one tile. `live_mask`: in each tile the live slots come first; every slot is live on each tile whose node row range and node column range meet.
All inputs are finite; a program needn't handle non-finite values.
Results may differ from the reference program's by a relative error of at most 0.0049.
Values may be sent and summed in bfloat16 or wider, within the bound.
A program may use at most 128 MiB of HBM per device.

```python
import math
import jax
import jax.numpy as jnp
from jax import lax

FEAT = 128
HIDDEN_SIZE = 256
BLK = 128
GRID_ROWS = 16
GRID_COLS = 16
NODES = 131072
TILE_ROWS = 64
TILE_COLS = 64
KMAX = 256
N_COL = 16


def slot_layout(key):
    tiles = GRID_ROWS * GRID_COLS
    positions = TILE_ROWS * TILE_COLS
    tile_keys = jax.random.split(jax.random.fold_in(key, 101), tiles)
    picked = jax.vmap(lambda tile_key: jax.random.permutation(tile_key, positions)[:KMAX])(tile_keys)
    picked = picked.reshape(GRID_ROWS, GRID_COLS, KMAX).astype(jnp.int32)
    row_index = jnp.arange(GRID_ROWS, dtype=jnp.int32)[:, None]
    col_index = jnp.arange(GRID_COLS, dtype=jnp.int32)[None, :]
    row_start = row_index * (TILE_ROWS * BLK)
    row_end = row_start + TILE_ROWS * BLK
    col_start = col_index * (TILE_COLS * BLK)
    col_end = col_start + TILE_COLS * BLK
    touching = (row_start < col_end) & (col_start < row_end)
    counts = jax.random.randint(jax.random.fold_in(key, 102), (GRID_ROWS, GRID_COLS), max(1, KMAX // 8), KMAX // 2 + 1, dtype=jnp.int32)
    counts = jnp.where(touching, KMAX, counts)
    live_slots = (jnp.arange(KMAX, dtype=jnp.int32)[None, None, :] < counts[:, :, None]).astype(jnp.int32)
    return (picked // TILE_COLS, picked % TILE_COLS, live_slots)


def draw_block_rows(key, part):
    row_ids, col_ids, live_slots = slot_layout(key)
    return row_ids


def draw_block_cols(key, part):
    row_ids, col_ids, live_slots = slot_layout(key)
    return col_ids


def draw_live_mask(key, part):
    row_ids, col_ids, live_slots = slot_layout(key)
    return live_slots


def block_scale(stream_key, shape, shards, smallest, high):
    loudness = 1.0
    for axis_at, blocks in shards:
        heights = jax.random.uniform(jax.random.fold_in(jax.random.fold_in(stream_key, 6), axis_at), (blocks,), jnp.float32, smallest / len(shards), high / len(shards))
        loudness = loudness * jnp.repeat(jnp.exp(heights), shape[axis_at] // blocks).reshape((-1,) + (1,) * (len(shape) - 1 - axis_at))
    return loudness


def gaussian(own_key, extent, width, most, pieces=(), held_as=jnp.bfloat16):
    values = jax.random.normal(own_key, extent, jnp.float32) * width
    if len(pieces) > 0:
        values = block_scale(own_key, extent, pieces, -0.22, 0.18) * values
    return jnp.clip(values, min=-most, max=most).astype(held_as)


def setup_inputs(seed: int = 0) -> dict:
    arg_keys = jax.random.split(jax.random.key(seed), 8)
    features = gaussian(arg_keys[0], (NODES, FEAT), 1.0, 6.0, ((0, 256),))
    weight = gaussian(arg_keys[1], (FEAT, HIDDEN_SIZE), FEAT ** -0.5, 0.5)
    cotangent = gaussian(arg_keys[2], (NODES, HIDDEN_SIZE), 1.0, 6.0, ((0, 256),))
    adj_blocks = gaussian(arg_keys[3], (GRID_ROWS, GRID_COLS, KMAX, BLK, BLK), (BLK * KMAX * N_COL // TILE_ROWS) ** -0.5, 0.0625, ((0, 16), (1, 16)))
    block_rows = draw_block_rows(jax.random.fold_in(arg_keys[7], 71), 0)
    block_cols = draw_block_cols(jax.random.fold_in(arg_keys[7], 71), 0)
    live_mask = draw_live_mask(jax.random.fold_in(arg_keys[7], 71), 0)
    return dict(features=features, weight=weight, cotangent=cotangent, adj_blocks=adj_blocks, block_rows=block_rows, block_cols=block_cols, live_mask=live_mask)


def tile_product(values, pick_ids, put_ids, live_slots, source, put_count, transpose):
    columns = source.shape[1]
    blocked = source.reshape(-1, BLK, columns)
    gathered = blocked[pick_ids]
    einsum_form = 'kji,kjw->kiw' if transpose else 'kij,kjw->kiw'
    product = jnp.einsum(einsum_form, values.astype(jnp.float32), gathered.astype(jnp.float32), precision=lax.Precision.HIGHEST)
    product = product * live_slots.astype(jnp.float32)[:, None, None]
    summed = jax.ops.segment_sum(product, put_ids, num_segments=put_count)
    return summed.reshape(put_count * BLK, columns)

def reference(features, weight, cotangent, adj_blocks, block_rows, block_cols, live_mask):
    span_rows = TILE_ROWS * BLK
    span_cols = TILE_COLS * BLK

    def forward_row(row_index):

        def add_tile(col_index, total):
            source = lax.dynamic_slice_in_dim(features, col_index * span_cols, span_cols, 0)
            return total + tile_product(adj_blocks[row_index, col_index], block_cols[row_index, col_index], block_rows[row_index, col_index], live_mask[row_index, col_index], source, TILE_ROWS, False)
        return lax.fori_loop(0, GRID_COLS, add_tile, jnp.zeros((span_rows, FEAT), jnp.float32))
    aggregated = lax.map(forward_row, jnp.arange(GRID_ROWS, dtype=jnp.int32)).reshape(NODES, FEAT)
    weight_wide = weight.astype(jnp.float32)
    pre = jnp.dot(aggregated, weight_wide, precision=lax.Precision.HIGHEST)
    activated = jax.nn.silu(pre).astype(jnp.bfloat16)
    sigmoid = jax.nn.sigmoid(pre)
    grad_pre = (cotangent.astype(jnp.float32) * sigmoid * (1.0 + pre * (1.0 - sigmoid))).astype(jnp.bfloat16)
    grad_weight = jnp.dot(aggregated.T, grad_pre.astype(jnp.float32), precision=lax.Precision.HIGHEST)
    grad_weight = grad_weight * (1.0 / math.sqrt(NODES))
    narrowed = jnp.dot(grad_pre, weight.T, preferred_element_type=jnp.float32)

    def backward_col(col_index):

        def add_tile(row_index, total):
            source = lax.dynamic_slice_in_dim(narrowed, row_index * span_rows, span_rows, 0)
            return total + tile_product(adj_blocks[row_index, col_index], block_rows[row_index, col_index], block_cols[row_index, col_index], live_mask[row_index, col_index], source, TILE_COLS, True)
        return lax.fori_loop(0, GRID_ROWS, add_tile, jnp.zeros((span_cols, FEAT), jnp.float32))
    grad_input = lax.map(backward_col, jnp.arange(GRID_COLS, dtype=jnp.int32)).reshape(NODES, FEAT)
    return (activated, grad_input.astype(jnp.bfloat16), grad_weight)
```

```python
import functools
import math

import jax
import jax.numpy as jnp
from jax import lax
from jax.experimental import pallas as pl
from jax.experimental.pallas import tpu as pltpu
from jax.sharding import PartitionSpec as P

MESH = pl.DeviceIdType.MESH
BF = jnp.bfloat16
F32 = jnp.float32
BLK = 128
SLOTS = 256
BLOCKS = 64
UNROLL = 32


def slot_tables(put, pick, live):
    shape = (SLOTS, SLOTS)
    put_lane = jnp.broadcast_to(jnp.where(live != 0, put, BLOCKS), shape)
    put_sub = put_lane.T
    pick_sub = jnp.broadcast_to(pick, shape).T
    sub = lax.broadcasted_iota(jnp.int32, shape, 0)
    lane = lax.broadcasted_iota(jnp.int32, shape, 1)

    def count(mask, axis):
        return jnp.sum(mask.astype(jnp.int32), axis=axis, keepdims=True)

    rank = count(put_lane * SLOTS + lane < put_sub * SLOTS + sub, 1)
    chosen = rank == lane
    continues = count((put_lane == put_sub) & (lane < sub), 1) > 0
    order = jnp.sum(jnp.where(chosen, sub, 0), axis=0, keepdims=True)
    source = jnp.sum(jnp.where(chosen, pick_sub, 0), axis=0, keepdims=True)
    follow = count(chosen & continues, 0)
    held = count(put_sub == lane, 0)
    upto = count(put_sub <= lane, 0)
    last = jnp.where(held > 0, upto - 1, SLOTS)
    return order, source, follow, last


def kernel(
    feat, weight, cot, adj, rows, cols, live,
    act_out, gi_out, gw_out,
    a_v, x_v, s_v, p_v, g_v, p2_v, w_v, cot_v, act_v, gp_v, hi_v, lo_v, gi_v,
    rl, rr, rxl, rxr, zs, rz, tz,
    sib, rl2, rr2, rxl2, rxr2, zs2, rz2,
    gwp, gx, g1, gz, gy, g3, gc, g4, gh, gwf,
    tab_v, tab, send_sem, recv_sem, local_sem,
):
    row = lax.axis_index("row")
    col = lax.axis_index("col")
    y, h, c = row // 4, (row // 2) % 2, row % 2
    x, z = col // 4, col % 4
    xr, xo, xl = (x + 1) % 4, (x + 2) % 4, (x + 3) % 4
    yr, yo, yl = (y + 1) % 4, (y + 2) % 4, (y + 3) % 4

    def col_dev(x_, z_):
        return (row, x_ * 4 + z_)

    def row_of(y_, h_, c_):
        return y_ * 4 + h_ * 2 + c_

    def row_dev(y_, h_, c_):
        return (row_of(y_, h_, c_), col)

    peers = [col_dev(xr, z), col_dev(xo, z), col_dev(xl, z)]
    peers += [col_dev(x, (z + d) % 4) for d in (1, 2, 3)]
    peers += [row_dev(yr, h, c), row_dev(yo, h, c), row_dev(yl, h, c)]
    peers += [row_dev(y, 1 - h, c), row_dev(y, h, 1 - c)]
    barrier = pltpu.get_barrier_semaphore()
    for peer in peers:
        pl.semaphore_signal(barrier, inc=1, device_id=peer, device_id_type=MESH)

    names = {}
    pending = []

    def number(name):
        return names.setdefault(name, len(names))

    def send(name, src, dst, device):
        k = number(name)
        copy = pltpu.make_async_remote_copy(
            src_ref=src, dst_ref=dst, send_sem=send_sem.at[k], recv_sem=recv_sem.at[k],
            device_id=device, device_id_type=MESH,
        )
        copy.start()
        pending.append(copy)

    def recv(name, dst, device):
        k = number(name)
        pltpu.make_async_remote_copy(
            src_ref=dst, dst_ref=dst, send_sem=send_sem.at[k], recv_sem=recv_sem.at[k],
            device_id=device, device_id_type=MESH,
        ).wait_recv()

    def flush():
        while pending:
            pending.pop(0).wait_send()

    load_a = pltpu.make_async_copy(adj, a_v, local_sem.at[0])
    load_a.start()
    load_w = pltpu.make_async_copy(weight, w_v, local_sem.at[1])
    load_w.start()
    load_c = pltpu.make_async_copy(cot, cot_v, local_sem.at[2])
    load_c.start()

    def part(ref, chunk, lo=0, hi=4):
        return ref.at[pl.ds(chunk * 4 + lo, hi - lo)]

    own = part(x_v, row)
    load_f = pltpu.make_async_copy(feat, own, local_sem.at[3])
    load_f.start()
    pl.semaphore_wait(barrier, len(peers))

    send("Az", feat, own, row_dev(y, 1 - h, c))
    send("Ar0", feat, own, row_dev(yr, h, c))
    send("Al0", feat, own, row_dev(yl, h, c))
    send("As", feat, own, row_dev(y, h, 1 - c))

    table = slot_tables(rows[...], cols[...], live[...])
    for k in range(4):
        tab_v[k : k + 1, :] = table[k]
    table = slot_tables(cols[...], rows[...], live[...])
    for k in range(4):
        tab_v[k + 4 : k + 5, :] = table[k]
    load_t = pltpu.make_async_copy(tab_v, tab, local_sem.at[4])
    load_t.start()
    s_v[SLOTS] = jnp.zeros((BLK, BLK), F32)

    sibling = row_dev(y, h, 1 - c)

    def share(name, chunk, lo=0, hi=4):
        send("S" + name, part(x_v, chunk, lo, hi), part(x_v, chunk, lo, hi), sibling)

    left, right = row_of(yl, h, c), row_of(yr, h, c)
    recv("Ar0", part(x_v, left), row_dev(yl, h, c))
    send("Arr", part(x_v, left, 0, 2), part(x_v, left, 0, 2), row_dev(yr, h, c))
    share("l0", left)
    recv("Al0", part(x_v, right), row_dev(yr, h, c))
    send("All", part(x_v, right, 2, 4), part(x_v, right, 2, 4), row_dev(yl, h, c))
    share("r0", right)
    across = row_of(y, 1 - h, c)
    recv("Az", part(x_v, across), row_dev(y, 1 - h, c))
    chunk = part(x_v, across)
    send("Ar1", chunk, chunk, row_dev(yr, h, c))
    send("Al1", chunk, chunk, row_dev(yl, h, c))
    send("Ao1", chunk, chunk, row_dev(yo, h, c))
    share("z", across)
    opp = row_of(yo, h, c)
    recv("Arr", part(x_v, opp, 0, 2), row_dev(yl, h, c))
    share("o0a", opp, 0, 2)
    recv("All", part(x_v, opp, 2, 4), row_dev(yr, h, c))
    share("o0b", opp, 2, 4)
    far = [row_of(yl, 1 - h, c), row_of(yr, 1 - h, c), row_of(yo, 1 - h, c)]
    recv("Ar1", part(x_v, far[0]), row_dev(yl, h, c))
    share("l1", far[0])
    recv("Al1", part(x_v, far[1]), row_dev(yr, h, c))
    share("r1", far[1])
    recv("Ao1", part(x_v, far[2]), row_dev(yo, h, c))
    share("o1", far[2])

    def shared(name, chunk, lo=0, hi=4):
        recv("S" + name, part(x_v, chunk, lo, hi), sibling)

    load_f.wait()
    load_t.wait()
    load_a.wait()
    d = 1 - c
    recv("As", part(x_v, row_of(y, h, d)), sibling)
    shared("l0", row_of(yl, h, d))
    shared("r0", row_of(yr, h, d))
    shared("z", row_of(y, 1 - h, d))
    shared("o0a", row_of(yo, h, d), 0, 2)
    shared("o0b", row_of(yo, h, d), 2, 4)
    shared("l1", row_of(yl, 1 - h, d))
    shared("r1", row_of(yr, 1 - h, d))
    shared("o1", row_of(yo, 1 - h, d))

    def spmm(base, source, adjacency_right):
        def step(k, total):
            block = a_v[tab[base, k]]
            other = source[tab[base + 1, k]]
            if adjacency_right:
                product = jnp.dot(other, block, preferred_element_type=F32)
            else:
                product = jnp.dot(block, other, preferred_element_type=F32)
            total = jnp.where(tab[base + 2, k] != 0, total, 0.0) + product
            s_v[k] = total
            return total

        lax.fori_loop(0, SLOTS, step, jnp.zeros((BLK, BLK), F32), unroll=UNROLL)

    spmm(0, x_v, False)

    def partial(chunk, b):
        return s_v[tab[3, chunk * 4 + b]]

    def each(lo, hi, body):
        def step(b, carry):
            body(b)
            return carry

        lax.fori_loop(lo, hi, step, 0)

    def fill(chunk, lo, hi):
        def body(b):
            p_v[chunk * 4 + b] = partial(chunk, b).astype(BF)

        each(lo, hi, body)

    zj = [(z + 1 + j) % 4 for j in range(4)]
    to_r, to_l = col_dev(xr, z), col_dev(xl, z)

    def relay(j):
        chunk = xo * 4 + zj[j]
        fill(chunk, 0, 4)
        send(f"Brr{j}", part(p_v, chunk, 0, 2), rl.at[j], to_r)
        send(f"Brl{j}", part(p_v, chunk, 2, 4), rr.at[j], to_l)

    def raw(j):
        chunk = xr * 4 + zj[j]
        fill(chunk, 2, 4)
        send(f"Bwr{j}", part(p_v, chunk, 2, 4), rxl.at[j, pl.ds(2, 2)], to_r)
        chunk = xl * 4 + zj[j]
        fill(chunk, 0, 2)
        send(f"Bwl{j}", part(p_v, chunk, 0, 2), rxr.at[j, pl.ds(0, 2)], to_l)

    def summed(j):
        chunk_r = xr * 4 + zj[j]
        recv(f"Brr{j}", rl.at[j], to_l)

        def body_r(b):
            p_v[chunk_r * 4 + b] = (partial(chunk_r, b) + rl[j, b].astype(F32)).astype(BF)

        each(0, 2, body_r)
        send(f"Bsr{j}", part(p_v, chunk_r, 0, 2), rxl.at[j, pl.ds(0, 2)], to_r)
        chunk_l = xl * 4 + zj[j]
        recv(f"Brl{j}", rr.at[j], to_r)

        def body_l(b):
            p_v[chunk_l * 4 + 2 + b] = (partial(chunk_l, b + 2) + rr[j, b].astype(F32)).astype(BF)

        each(0, 2, body_l)
        send(f"Bsl{j}", part(p_v, chunk_l, 2, 4), rxr.at[j, pl.ds(2, 2)], to_l)

    def finish(j):
        recv(f"Bwr{j}", rxl.at[j, pl.ds(2, 2)], to_l)
        recv(f"Bwl{j}", rxr.at[j, pl.ds(0, 2)], to_r)
        recv(f"Bsr{j}", rxl.at[j, pl.ds(0, 2)], to_l)
        recv(f"Bsl{j}", rxr.at[j, pl.ds(2, 2)], to_r)
        chunk = x * 4 + zj[j]

        def body(b):
            total = partial(chunk, b) + rxl[j, b].astype(F32) + rxr[j, b].astype(F32)
            if j < 3:
                zs[j, b] = total.astype(BF)
            else:
                tz[b] = total

        each(0, 4, body)
        if j < 3:
            send(f"Bz{j}", zs.at[j], rz.at[j], col_dev(x, zj[j]))

    relay(0)
    raw(0)
    relay(1)
    for j in range(4):
        summed(j)
        if j < 3:
            raw(j + 1)
        if j < 2:
            relay(j + 2)
        if j > 0:
            finish(j - 1)
    finish(3)
    load_w.wait()
    load_c.wait()
    for j in range(3):
        recv(f"Bz{j}", rz.at[j], col_dev(x, (z + 3 - j) % 4))

    def layer(b):
        agg = tz[b] + rz[0, b].astype(F32) + rz[1, b].astype(F32) + rz[2, b].astype(F32)
        high = agg.astype(BF)
        low = (agg - high.astype(F32)).astype(BF)
        hi_v[b] = high
        lo_v[b] = low
        w = w_v[...]
        pre = jnp.dot(high, w, preferred_element_type=F32) + jnp.dot(low, w, preferred_element_type=F32)
        s = lax.logistic(pre)
        act_v[b] = (pre * s).astype(BF)
        grad = (cot_v[b].astype(F32) * s * (1.0 + pre * (1.0 - s))).astype(BF)
        gp_v[b] = grad
        narrow = lax.dot_general(w, grad, (((1,), (1,)), ((), ())), preferred_element_type=F32)
        g_v[col * 4 + b] = narrow.astype(BF)

    each(0, 4, layer)

    zsrc = [z, (z + 3) % 4, (z + 1) % 4, (z + 2) % 4]
    zdst = [z, (z + 1) % 4, (z + 3) % 4, (z + 2) % 4]

    def along(s):
        chunk = part(g_v, x * 4 + zsrc[s])
        send(f"Cr{s}", chunk, chunk, to_r)
        send(f"Cl{s}", chunk, chunk, to_l)

    def pass_on(s):
        chunk = xl * 4 + zsrc[s]
        recv(f"Cr{s}", part(g_v, chunk), to_l)
        send(f"Crr{s}", part(g_v, chunk, 0, 2), part(g_v, chunk, 0, 2), to_r)
        chunk = xr * 4 + zsrc[s]
        recv(f"Cl{s}", part(g_v, chunk), to_r)
        send(f"Cll{s}", part(g_v, chunk, 2, 4), part(g_v, chunk, 2, 4), to_l)

    along(0)
    mine = part(g_v, col)
    for s in (1, 2, 3):
        send(f"Cz{s}", mine, mine, col_dev(x, zdst[s]))
    store_a = pltpu.make_async_copy(act_v, act_out, local_sem.at[5])
    store_a.start()

    gwp[...] = jnp.zeros_like(gwp)

    def weight_term(b):
        dims = (((0,), (0,)), ((), ()))
        grad = gp_v[b]
        gwp[...] += lax.dot_general(hi_v[b], grad, dims, preferred_element_type=F32) + lax.dot_general(
            lo_v[b], grad, dims, preferred_element_type=F32
        )

    each(0, 4, weight_term)
    for k in (1, 2, 3):
        to = (x + k) % 4
        send(f"Gx{k}", gwp.at[pl.ds(pl.multiple_of(to * 32, 32), 32)], gx.at[k - 1], col_dev(to, z))

    def arrive(s):
        chunk = part(g_v, x * 4 + zsrc[s])
        recv(f"Cz{s}", chunk, col_dev(x, zsrc[s]))

    arrive(1)
    along(1)
    pass_on(0)
    for k in (1, 2, 3):
        recv(f"Gx{k}", gx.at[k - 1], col_dev((x + 4 - k) % 4, z))
    g1[...] = gwp[pl.ds(pl.multiple_of(x * 32, 32), 32), :] + gx[0] + gx[1] + gx[2]
    for k in (1, 2, 3):
        to = (z + k) % 4
        send(f"Gz{k}", g1.at[pl.ds(pl.multiple_of(to * 8, 8), 8)], gz.at[k - 1], col_dev(x, to))
    arrive(2)
    along(2)
    pass_on(1)
    for k in (1, 2, 3):
        recv(f"Gz{k}", gz.at[k - 1], col_dev(x, (z + 4 - k) % 4))
    gy[y] = g1[pl.ds(pl.multiple_of(z * 8, 8), 8), :] + gz[0] + gz[1] + gz[2]
    for k in (1, 2, 3):
        send(f"Gy{k}", gy.at[y], gy.at[y], row_dev((y + k) % 4, h, c))
    arrive(3)
    along(3)
    pass_on(2)
    for k in (1, 2, 3):
        frm = (y + 4 - k) % 4
        recv(f"Gy{k}", gy.at[frm], row_dev(frm, h, c))
    g3[...] = gy[0] + gy[1] + gy[2] + gy[3]
    send("Gc", g3, gc, sibling)
    pass_on(3)
    recv("Gc", gc, sibling)
    g4[...] = g3[...] + gc[...]
    across_dev = row_dev(y, 1 - h, c)
    send("Gh", g4, gh, across_dev)
    for s in range(4):
        chunk = xo * 4 + zsrc[s]
        recv(f"Crr{s}", part(g_v, chunk, 0, 2), to_l)
        recv(f"Cll{s}", part(g_v, chunk, 2, 4), to_r)

    spmm(4, g_v, True)

    recv("Gh", gh, across_dev)
    at = pl.multiple_of(x * 32 + z * 8, 8)
    scale = 1.0 / math.sqrt(BLK * BLOCKS * 16)
    gwf[pl.ds(at, 8), :] = (g4[...] + gh[...]) * scale
    for k in (1, 2, 3):
        piece = gwf.at[pl.ds(at, 8)]
        send(f"Gu{k}", piece, piece, col_dev(x, (z + k) % 4))

    def partial2(chunk, b):
        return s_v[tab[7, chunk * 4 + b]]

    order = [(y_, h_) for h_ in (1 - h, h) for y_ in (yo, yr, yl, y)]
    for i, (y_, h_) in enumerate(order):
        chunk = row_of(y_, h_, 1 - c)

        def body(b, chunk=chunk):
            p2_v[chunk * 4 + b] = partial2(chunk, b).astype(BF)

        each(0, 4, body)
        send(f"Es{i}", part(p2_v, chunk), sib.at[i], sibling)

    def both(i, chunk, b):
        return partial2(chunk, b) + sib[i, b].astype(F32)

    up, down = row_dev(yr, h, c), row_dev(yl, h, c)

    def chunk_of(i):
        return row_of(order[i][0], order[i][1], c)

    def store_both(i, lo, hi):
        chunk = chunk_of(i)

        def body(b):
            p2_v[chunk * 4 + b] = both(i, chunk, b).astype(BF)

        each(lo, hi, body)

    def relay2(g):
        i = 4 * g
        recv(f"Es{i}", sib.at[i], sibling)
        store_both(i, 0, 4)
        send(f"Err{g}", part(p2_v, chunk_of(i), 0, 2), rl2.at[g], up)
        send(f"Erl{g}", part(p2_v, chunk_of(i), 2, 4), rr2.at[g], down)

    def raw2(g):
        i = 4 * g + 1
        recv(f"Es{i}", sib.at[i], sibling)
        store_both(i, 2, 4)
        send(f"Ewr{g}", part(p2_v, chunk_of(i), 2, 4), rxl2.at[g, pl.ds(2, 2)], up)
        i = 4 * g + 2
        recv(f"Es{i}", sib.at[i], sibling)
        store_both(i, 0, 2)
        send(f"Ewl{g}", part(p2_v, chunk_of(i), 0, 2), rxr2.at[g, pl.ds(0, 2)], down)

    def summed2(g):
        i = 4 * g + 1
        chunk_r = chunk_of(i)
        recv(f"Err{g}", rl2.at[g], down)

        def body_r(b):
            p2_v[chunk_r * 4 + b] = (both(i, chunk_r, b) + rl2[g, b].astype(F32)).astype(BF)

        each(0, 2, body_r)
        send(f"Esr{g}", part(p2_v, chunk_r, 0, 2), rxl2.at[g, pl.ds(0, 2)], up)
        i2 = 4 * g + 2
        chunk_l = chunk_of(i2)
        recv(f"Erl{g}", rr2.at[g], up)

        def body_l(b):
            p2_v[chunk_l * 4 + 2 + b] = (both(i2, chunk_l, b + 2) + rr2[g, b].astype(F32)).astype(BF)

        each(0, 2, body_l)
        send(f"Esl{g}", part(p2_v, chunk_l, 2, 4), rxr2.at[g, pl.ds(2, 2)], down)

    def gathered2(g):
        i = 4 * g + 3
        recv(f"Es{i}", sib.at[i], sibling)
        recv(f"Ewr{g}", rxl2.at[g, pl.ds(2, 2)], down)
        recv(f"Ewl{g}", rxr2.at[g, pl.ds(0, 2)], up)
        recv(f"Esr{g}", rxl2.at[g, pl.ds(0, 2)], down)
        recv(f"Esl{g}", rxr2.at[g, pl.ds(2, 2)], up)
        chunk = chunk_of(i)

        def total(b):
            return both(i, chunk, b) + rxl2[g, b].astype(F32) + rxr2[g, b].astype(F32)

        return total

    relay2(0)
    raw2(0)
    relay2(1)
    summed2(0)
    raw2(1)
    total = gathered2(0)

    def to_across(b):
        zs2[b] = total(b).astype(BF)

    each(0, 4, to_across)
    send("Ez", zs2, rz2, across_dev)
    summed2(1)
    for k in (1, 2, 3):
        frm = (z + 4 - k) % 4
        recv(f"Gu{k}", gwf.at[pl.ds(pl.multiple_of(x * 32 + frm * 8, 8), 8)], col_dev(x, frm))
    for k in (1, 2, 3):
        piece = gwf.at[pl.ds(pl.multiple_of(x * 32, 32), 32)]
        send(f"Gv{k}", piece, piece, col_dev((x + k) % 4, z))
    total2 = gathered2(1)
    flush_before = list(pending)
    del pending[:]
    for copy in flush_before:
        copy.wait_send()
    recv("Ez", rz2, across_dev)

    def output(b):
        gi_v[b] = (total2(b) + rz2[b].astype(F32)).T.astype(BF)

    each(0, 4, output)
    store_i = pltpu.make_async_copy(gi_v, gi_out, local_sem.at[6])
    store_i.start()
    for k in (1, 2, 3):
        frm = (x + 4 - k) % 4
        recv(f"Gv{k}", gwf.at[pl.ds(pl.multiple_of(frm * 32, 32), 32)], col_dev(frm, z))
    store_w = pltpu.make_async_copy(gwf, gw_out, local_sem.at[7])
    store_w.start()
    flush()
    store_a.wait()
    store_i.wait()
    store_w.wait()


def on_device(features, weight, cotangent, adj_blocks, block_rows, block_cols, live_mask):
    hbm = pl.BlockSpec(memory_space=pl.ANY)
    vmem = pl.BlockSpec(memory_space=pltpu.VMEM)
    quad = (4, BLK, BLK)
    scratch = [
        pltpu.VMEM((SLOTS, BLK, BLK), BF),
        pltpu.VMEM((BLOCKS, BLK, BLK), BF),
        pltpu.VMEM((SLOTS + 1, BLK, BLK), F32),
        pltpu.VMEM((BLOCKS, BLK, BLK), BF),
        pltpu.VMEM((BLOCKS, BLK, BLK), BF),
        pltpu.VMEM((BLOCKS, BLK, BLK), BF),
        pltpu.VMEM((BLK, 2 * BLK), BF),
        pltpu.VMEM((4, BLK, 2 * BLK), BF),
        pltpu.VMEM((4, BLK, 2 * BLK), BF),
        pltpu.VMEM((4, BLK, 2 * BLK), BF),
        pltpu.VMEM(quad, BF),
        pltpu.VMEM(quad, BF),
        pltpu.VMEM(quad, BF),
        pltpu.VMEM((4, 2, BLK, BLK), BF),
        pltpu.VMEM((4, 2, BLK, BLK), BF),
        pltpu.VMEM((4,) + quad, BF),
        pltpu.VMEM((4,) + quad, BF),
        pltpu.VMEM((3,) + quad, BF),
        pltpu.VMEM((3,) + quad, BF),
        pltpu.VMEM(quad, F32),
        pltpu.VMEM((8,) + quad, BF),
        pltpu.VMEM((2, 2, BLK, BLK), BF),
        pltpu.VMEM((2, 2, BLK, BLK), BF),
        pltpu.VMEM((2,) + quad, BF),
        pltpu.VMEM((2,) + quad, BF),
        pltpu.VMEM(quad, BF),
        pltpu.VMEM(quad, BF),
        pltpu.VMEM((BLK, 2 * BLK), F32),
        pltpu.VMEM((3, 32, 2 * BLK), F32),
        pltpu.VMEM((32, 2 * BLK), F32),
        pltpu.VMEM((3, 8, 2 * BLK), F32),
        pltpu.VMEM((4, 8, 2 * BLK), F32),
        pltpu.VMEM((8, 2 * BLK), F32),
        pltpu.VMEM((8, 2 * BLK), F32),
        pltpu.VMEM((8, 2 * BLK), F32),
        pltpu.VMEM((8, 2 * BLK), F32),
        pltpu.VMEM((BLK, 2 * BLK), F32),
        pltpu.VMEM((8, SLOTS), jnp.int32),
        pltpu.SMEM((8, SLOTS), jnp.int32),
        pltpu.SemaphoreType.DMA((128,)),
        pltpu.SemaphoreType.DMA((128,)),
        pltpu.SemaphoreType.DMA((8,)),
    ]
    act, gi, gw = pl.pallas_call(
        kernel,
        out_shape=(
            jax.ShapeDtypeStruct((4, BLK, 2 * BLK), BF),
            jax.ShapeDtypeStruct(quad, BF),
            jax.ShapeDtypeStruct((BLK, 2 * BLK), F32),
        ),
        in_specs=[hbm, hbm, hbm, hbm, vmem, vmem, vmem],
        out_specs=(hbm, hbm, hbm),
        scratch_shapes=scratch,
        compiler_params=pltpu.CompilerParams(
            collective_id=0, has_side_effects=True, vmem_limit_bytes=60 << 20
        ),
        cost_estimate=pl.CostEstimate(flops=2 << 30, bytes_accessed=12 << 20, transcendentals=1 << 17),
        name="graph_layer",
    )(
        features.reshape(quad),
        weight,
        cotangent.reshape(4, BLK, 2 * BLK),
        adj_blocks.reshape(SLOTS, BLK, BLK),
        block_rows.reshape(1, SLOTS),
        block_cols.reshape(1, SLOTS),
        live_mask.reshape(1, SLOTS),
    )
    return act.reshape(4 * BLK, 2 * BLK), gi.reshape(4 * BLK, BLK), gw


def solution(mesh):
    in_specs = (
        P(("col", "row"), None),
        P(),
        P(("row", "col"), None),
        P("row", "col", None, None, None),
        P("row", "col", None),
        P("row", "col", None),
        P("row", "col", None),
    )
    out_specs = (P(("row", "col"), None), P(("col", "row"), None), P())
    return jax.shard_map(
        on_device, mesh=mesh, in_specs=in_specs, out_specs=out_specs, check_vma=False
    )
```

```python
import functools
import math

import jax
import jax.numpy as jnp
from jax import lax
from jax.experimental import pallas as pl
from jax.experimental.pallas import tpu as pltpu
from jax.sharding import PartitionSpec as P

MESH = pl.DeviceIdType.MESH
BF = jnp.bfloat16
F32 = jnp.float32
BLK = 128
SLOTS = 256
BLOCKS = 64
HALF = 64
STRAIGHT = ((0, 3), (1, 2), (1, 3))
UNROLL = 64


def slot_tables(put, pick, live):
    shape = (SLOTS, SLOTS)
    put_lane = jnp.broadcast_to(jnp.where(live != 0, put, BLOCKS), shape)
    put_sub = put_lane.T
    pick_sub = jnp.broadcast_to(pick, shape).T
    sub = lax.broadcasted_iota(jnp.int32, shape, 0)
    lane = lax.broadcasted_iota(jnp.int32, shape, 1)

    def count(mask, axis):
        return jnp.sum(mask.astype(jnp.int32), axis=axis, keepdims=True)

    rank = count(put_lane * SLOTS + lane < put_sub * SLOTS + sub, 1)
    chosen = rank == lane
    continues = count((put_lane == put_sub) & (lane < sub), 1) > 0
    order = jnp.sum(jnp.where(chosen, sub, 0), axis=0, keepdims=True)
    source = jnp.sum(jnp.where(chosen, pick_sub, 0), axis=0, keepdims=True)
    follow = count(chosen & continues, 0)
    held = count(put_sub == lane, 0)
    upto = count(put_sub <= lane, 0)
    last = jnp.where(held > 0, upto - 1, SLOTS)
    return order, source, follow, last


def kernel(
    feat, weight, cot, adj, rows, cols, live,
    act_out, gi_out, gw_out,
    a_v, at_v, f_v, x_0, x_1, s_v, p_v, g_0, g_1, p2_v, w_v, cot_v, act_v, gp_v, hi_v, lo_v, gi_v,
    rl, rr, rxl, rxr, zs, rz, tz,
    sib, rl2, rr2, rxl2, rxr2, zs2, rz2,
    gwp, gx, g1, gz, gy, g3, gc, g4, gh, gwf,
    tab_v, tab, send_sem, recv_sem, local_sem,
):
    row = lax.axis_index("row")
    col = lax.axis_index("col")
    y, h, c = row // 4, (row // 2) % 2, row % 2
    x, z = col // 4, col % 4
    xr, xo, xl = (x + 1) % 4, (x + 2) % 4, (x + 3) % 4
    yr, yo, yl = (y + 1) % 4, (y + 2) % 4, (y + 3) % 4

    def col_dev(x_, z_):
        return (row, x_ * 4 + z_)

    def row_of(y_, h_, c_):
        return y_ * 4 + h_ * 2 + c_

    def row_dev(y_, h_, c_):
        return (row_of(y_, h_, c_), col)

    x_v, g_v = (x_0, x_1), (g_0, g_1)
    to_r, to_l, to_o = col_dev(xr, z), col_dev(xl, z), col_dev(xo, z)
    up, down, over = row_dev(yr, h, c), row_dev(yl, h, c), row_dev(yo, h, c)
    across_dev, sibling = row_dev(y, 1 - h, c), row_dev(y, h, 1 - c)

    peers = [to_r, col_dev(xo, z), to_l]
    peers += [col_dev(x, (z + d) % 4) for d in (1, 2, 3)]
    peers += [up, over, down, across_dev, sibling]
    barrier = pltpu.get_barrier_semaphore()
    for peer in peers:
        pl.semaphore_signal(barrier, inc=1, device_id=peer, device_id_type=MESH)

    names = {}
    pending = []

    def number(name):
        return names.setdefault(name, len(names))

    def send(name, src, dst, device):
        k = number(name)
        copy = pltpu.make_async_remote_copy(
            src_ref=src, dst_ref=dst, send_sem=send_sem.at[k], recv_sem=recv_sem.at[k],
            device_id=device, device_id_type=MESH,
        )
        copy.start()
        pending.append(copy)

    def recv(name, dst, device):
        k = number(name)
        pltpu.make_async_remote_copy(
            src_ref=dst, dst_ref=dst, send_sem=send_sem.at[k], recv_sem=recv_sem.at[k],
            device_id=device, device_id_type=MESH,
        ).wait_recv()

    def flush(copies):
        for copy in copies:
            copy.wait_send()

    def taken():
        copies = list(pending)
        del pending[:]
        return copies

    def each(lo, hi, body):
        def step(b, carry):
            body(b)
            return carry

        lax.fori_loop(lo, hi, step, 0, unroll=hi - lo)

    load_f = pltpu.make_async_copy(feat, f_v, local_sem.at[3])
    load_f.start()
    load_a = pltpu.make_async_copy(adj, a_v, local_sem.at[0])
    load_a.start()
    load_w = pltpu.make_async_copy(weight, w_v, local_sem.at[1])
    load_w.start()
    load_c = pltpu.make_async_copy(cot, cot_v, local_sem.at[2])
    load_c.start()

    def part(ref, f, chunk, lo=0, hi=4):
        at = pl.ds(chunk * 4 + lo, hi - lo)
        return ref[f].at[at] if isinstance(ref, tuple) else ref.at[f, at]

    load_f.wait()

    def turn(b):
        turned = f_v[b].T
        x_0[row * 4 + b] = turned[:HALF]
        x_1[row * 4 + b] = turned[HALF:]

    each(0, 4, turn)
    pl.semaphore_wait(barrier, len(peers))

    def begin(f):
        own = part(x_v, f, row)
        send(f"Az{f}", own, own, across_dev)
        send(f"Ar{f}", own, own, up)
        send(f"Al{f}", own, own, down)
        send(f"As{f}", own, own, sibling)

    begin(0)
    table = slot_tables(rows[...], cols[...], live[...])
    for k in range(4):
        tab_v[k : k + 1, :] = table[k]
    table = slot_tables(cols[...], rows[...], live[...])
    for k in range(4):
        tab_v[k + 4 : k + 5, :] = table[k]
    load_t = pltpu.make_async_copy(tab_v, tab, local_sem.at[4])
    load_t.start()
    for f in range(2):
        s_v[f, SLOTS] = jnp.zeros((HALF, BLK), F32)

    def share(name, f, chunk, lo=0, hi=4):
        send("S" + name, part(x_v, f, chunk, lo, hi), part(x_v, f, chunk, lo, hi), sibling)

    left, right, opp = row_of(yl, h, c), row_of(yr, h, c), row_of(yo, h, c)
    across = row_of(y, 1 - h, c)
    far = [row_of(yl, 1 - h, c), row_of(yr, 1 - h, c), row_of(yo, 1 - h, c)]

    def beside(f):
        recv(f"Ar{f}", part(x_v, f, left), down)
        send(f"Arr{f}", part(x_v, f, left, 0, 2), part(x_v, f, left, 0, 2), up)
        share(f"l{f}", f, left)
        recv(f"Al{f}", part(x_v, f, right), up)
        send(f"All{f}", part(x_v, f, right, 2, 4), part(x_v, f, right, 2, 4), down)
        share(f"r{f}", f, right)

    def crossed(f):
        piece = part(x_v, f, across)
        recv(f"Az{f}", piece, across_dev)
        send(f"Afr{f}", piece, piece, up)
        send(f"Afl{f}", piece, piece, down)
        send(f"Afo{f}", piece, piece, over)
        share(f"z{f}", f, across)

    def opposite(f):
        recv(f"Arr{f}", part(x_v, f, opp, 0, 2), down)
        share(f"oa{f}", f, opp, 0, 2)
        recv(f"All{f}", part(x_v, f, opp, 2, 4), up)
        share(f"ob{f}", f, opp, 2, 4)

    def remote(f):
        recv(f"Afr{f}", part(x_v, f, far[0]), down)
        share(f"fl{f}", f, far[0])
        recv(f"Afl{f}", part(x_v, f, far[1]), up)
        share(f"fr{f}", f, far[1])
        recv(f"Afo{f}", part(x_v, f, far[2]), over)
        share(f"fo{f}", f, far[2])

    def shared(f):
        d = 1 - c

        def take(name, chunk, lo=0, hi=4):
            recv(name, part(x_v, f, chunk, lo, hi), sibling)

        take(f"As{f}", row_of(y, h, d))
        take(f"Sl{f}", row_of(yl, h, d))
        take(f"Sr{f}", row_of(yr, h, d))
        take(f"Sz{f}", row_of(y, 1 - h, d))
        take(f"Soa{f}", row_of(yo, h, d), 0, 2)
        take(f"Sob{f}", row_of(yo, h, d), 2, 4)
        take(f"Sfl{f}", row_of(yl, 1 - h, d))
        take(f"Sfr{f}", row_of(yr, 1 - h, d))
        take(f"Sfo{f}", row_of(yo, 1 - h, d))

    def turn_blocks(n):
        def step(k, carry):
            at_v[k] = a_v[k].T
            return carry

        lax.fori_loop(64 * n, 64 * n + 64, step, 0, unroll=16)

    def spmm(f, base, source, blocks):
        def step(k, total):
            block = blocks[tab[base, k]]
            other = source[f][tab[base + 1, k]]
            product = jnp.dot(other, block, preferred_element_type=F32)
            total = jnp.where(tab[base + 2, k] != 0, total, 0.0) + product
            s_v[f, k] = total
            return total

        held = [jnp.zeros((HALF, BLK), F32)]

        def quarter(n):
            held[0] = lax.fori_loop(64 * n, 64 * n + 64, step, held[0], unroll=64)

        return quarter

    beside(0)
    begin(1)
    crossed(0)
    load_a.wait()
    turn_blocks(0)
    opposite(0)
    beside(1)
    turn_blocks(1)
    crossed(1)
    turn_blocks(2)
    remote(0)
    turn_blocks(3)
    opposite(1)
    load_t.wait()
    shared(0)
    quarter = spmm(0, 0, x_v, at_v)
    for n in range(4):
        quarter(n)

    def partial(f, chunk, b):
        return s_v[f, tab[3, chunk * 4 + b]]

    def fill(f, chunk, lo, hi):
        def body(b):
            p_v[f, chunk * 4 + b] = partial(f, chunk, b).astype(BF)

        each(lo, hi, body)

    zj = [(z + 1 + j) % 4 for j in range(4)]

    def pair(ref, f, j, lo):
        return ref.at[f, j, pl.ds(lo, 2)]

    def relay(f, j):
        chunk = xo * 4 + zj[j]
        fill(f, chunk, 0, 4)
        send(f"Brr{f}{j}", part(p_v, f, chunk, 0, 2), rl.at[f, j], to_r)
        send(f"Brl{f}{j}", part(p_v, f, chunk, 2, 4), rr.at[f, j], to_l)

    def raw(f, j):
        chunk = xr * 4 + zj[j]
        fill(f, chunk, 2, 4)
        send(f"Bwr{f}{j}", part(p_v, f, chunk, 2, 4), pair(rxl, f, j, 2), to_r)
        chunk = xl * 4 + zj[j]
        fill(f, chunk, 0, 2)
        send(f"Bwl{f}{j}", part(p_v, f, chunk, 0, 2), pair(rxr, f, j, 0), to_l)

    def summed(f, j):
        chunk_r = xr * 4 + zj[j]
        recv(f"Brr{f}{j}", rl.at[f, j], to_l)

        def body_r(b):
            p_v[f, chunk_r * 4 + b] = (partial(f, chunk_r, b) + rl[f, j, b].astype(F32)).astype(BF)

        each(0, 2, body_r)
        send(f"Bsr{f}{j}", part(p_v, f, chunk_r, 0, 2), pair(rxl, f, j, 0), to_r)
        chunk_l = xl * 4 + zj[j]
        recv(f"Brl{f}{j}", rr.at[f, j], to_r)

        def body_l(b):
            p_v[f, chunk_l * 4 + 2 + b] = (
                partial(f, chunk_l, b + 2) + rr[f, j, b].astype(F32)
            ).astype(BF)

        each(0, 2, body_l)
        send(f"Bsl{f}{j}", part(p_v, f, chunk_l, 2, 4), pair(rxr, f, j, 2), to_l)

    def finish(f, j):
        recv(f"Bwr{f}{j}", pair(rxl, f, j, 2), to_l)
        recv(f"Bwl{f}{j}", pair(rxr, f, j, 0), to_r)
        recv(f"Bsr{f}{j}", pair(rxl, f, j, 0), to_l)
        recv(f"Bsl{f}{j}", pair(rxr, f, j, 2), to_r)
        chunk = x * 4 + zj[j]

        def body(b):
            total = partial(f, chunk, b) + rxl[f, j, b].astype(F32) + rxr[f, j, b].astype(F32)
            if j < 3:
                zs[f, j, b] = total.astype(BF)
            else:
                tz[f, b] = total

        each(0, 4, body)
        if j < 3:
            send(f"Bz{f}{j}", zs.at[f, j], rz.at[f, j], col_dev(x, zj[j]))

    quarter = spmm(1, 0, x_v, at_v)
    relay(0, 0)
    raw(0, 0)
    relay(0, 1)
    remote(1)
    summed(0, 0)
    raw(0, 1)
    relay(0, 2)
    shared(1)
    quarter(0)
    summed(0, 1)
    raw(0, 2)
    relay(0, 3)
    quarter(1)
    finish(0, 0)
    raw(0, 3)
    quarter(2)
    summed(0, 2)
    finish(0, 1)
    quarter(3)
    relay(1, 0)
    summed(0, 3)
    raw(1, 0)
    relay(1, 1)
    finish(0, 2)
    done = taken()
    summed(1, 0)
    raw(1, 1)
    relay(1, 2)
    finish(0, 3)
    summed(1, 1)
    raw(1, 2)
    relay(1, 3)
    finish(1, 0)
    summed(1, 2)
    raw(1, 3)
    finish(1, 1)
    summed(1, 3)
    flush(done)
    finish(1, 2)
    load_w.wait()
    load_c.wait()
    finish(1, 3)
    for f in range(2):
        for j in range(3):
            recv(f"Bz{f}{j}", rz.at[f, j], col_dev(x, (z + 3 - j) % 4))

    def layer(b):
        agg = jnp.concatenate(
            [
                tz[f, b] + rz[f, 0, b].astype(F32) + rz[f, 1, b].astype(F32) + rz[f, 2, b].astype(F32)
                for f in range(2)
            ],
            axis=0,
        ).T
        high = agg.astype(BF)
        low = (agg - high.astype(F32)).astype(BF)
        hi_v[b] = high
        lo_v[b] = low
        w = w_v[...]
        pre = jnp.dot(high, w, preferred_element_type=F32) + jnp.dot(low, w, preferred_element_type=F32)
        s = lax.logistic(pre)
        act_v[b] = (pre * s).astype(BF)
        grad = (cot_v[b].astype(F32) * s * (1.0 + pre * (1.0 - s))).astype(BF)
        gp_v[b] = grad
        narrow = lax.dot_general(w, grad, (((1,), (1,)), ((), ())), preferred_element_type=F32)
        narrow = narrow.astype(BF)
        g_0[col * 4 + b] = narrow[:HALF]
        g_1[col * 4 + b] = narrow[HALF:]

    each(0, 4, layer)

    zsrc = [z, (z + 3) % 4, (z + 1) % 4, (z + 2) % 4]
    zdst = [z, (z + 1) % 4, (z + 3) % 4, (z + 2) % 4]

    def along(f, s):
        chunk = part(g_v, f, x * 4 + zsrc[s])
        if s > 0:
            recv(f"Cz{f}{s}", chunk, col_dev(x, zsrc[s]))
        send(f"Cr{f}{s}", chunk, chunk, to_r)
        send(f"Cl{f}{s}", chunk, chunk, to_l)
        if (f, s) in STRAIGHT:
            send(f"Co{f}{s}", chunk, chunk, to_o)

    def pass_on(f, s):
        chunk = xl * 4 + zsrc[s]
        recv(f"Cr{f}{s}", part(g_v, f, chunk), to_l)
        if (f, s) not in STRAIGHT:
            send(f"Crr{f}{s}", part(g_v, f, chunk, 0, 2), part(g_v, f, chunk, 0, 2), to_r)
        chunk = xr * 4 + zsrc[s]
        recv(f"Cl{f}{s}", part(g_v, f, chunk), to_r)
        if (f, s) not in STRAIGHT:
            send(f"Cll{f}{s}", part(g_v, f, chunk, 2, 4), part(g_v, f, chunk, 2, 4), to_l)

    def passed(f):
        for s in range(4):
            chunk = xo * 4 + zsrc[s]
            if (f, s) in STRAIGHT:
                recv(f"Co{f}{s}", part(g_v, f, chunk), to_o)
            else:
                recv(f"Crr{f}{s}", part(g_v, f, chunk, 0, 2), to_l)
                recv(f"Cll{f}{s}", part(g_v, f, chunk, 2, 4), to_r)

    def beyond(f, s):
        mine = part(g_v, f, col)
        send(f"Cz{f}{s}", mine, mine, col_dev(x, zdst[s]))

    along(0, 0)
    beyond(0, 1)
    beyond(0, 2)
    along(1, 0)
    store_a = pltpu.make_async_copy(act_v, act_out, local_sem.at[5])
    store_a.start()

    gwp[...] = jnp.zeros_like(gwp)

    def weight_term(b):
        dims = (((0,), (0,)), ((), ()))
        grad = gp_v[b]
        gwp[...] += lax.dot_general(hi_v[b], grad, dims, preferred_element_type=F32) + lax.dot_general(
            lo_v[b], grad, dims, preferred_element_type=F32
        )

    each(0, 4, weight_term)
    for k in (1, 2, 3):
        to = (x + k) % 4
        send(f"Gx{k}", gwp.at[pl.ds(pl.multiple_of(to * 32, 32), 32)], gx.at[k - 1], col_dev(to, z))

    along(0, 1)
    beyond(0, 3)
    along(0, 2)
    beyond(1, 1)
    beyond(1, 2)
    pass_on(0, 0)
    for k in (1, 2, 3):
        recv(f"Gx{k}", gx.at[k - 1], col_dev((x + 4 - k) % 4, z))
    g1[...] = gwp[pl.ds(pl.multiple_of(x * 32, 32), 32), :] + gx[0] + gx[1] + gx[2]
    for k in (1, 2, 3):
        to = (z + k) % 4
        send(f"Gz{k}", g1.at[pl.ds(pl.multiple_of(to * 8, 8), 8)], gz.at[k - 1], col_dev(x, to))
    along(0, 3)
    pass_on(0, 1)
    along(1, 1)
    beyond(1, 3)
    pass_on(0, 2)
    along(1, 2)
    pass_on(1, 0)
    for k in (1, 2, 3):
        recv(f"Gz{k}", gz.at[k - 1], col_dev(x, (z + 4 - k) % 4))
    gy[y] = g1[pl.ds(pl.multiple_of(z * 8, 8), 8), :] + gz[0] + gz[1] + gz[2]
    for k in (1, 2, 3):
        send(f"Gy{k}", gy.at[y], gy.at[y], row_dev((y + k) % 4, h, c))
    pass_on(0, 3)
    along(1, 3)
    passed(0)

    quarter = spmm(0, 4, g_v, a_v)
    quarter(0)
    pass_on(1, 1)
    quarter(1)
    pass_on(1, 2)
    quarter(2)
    quarter(3)
    pass_on(1, 3)

    def partial2(f, chunk, b):
        return s_v[f, tab[7, chunk * 4 + b]]

    order = [(y_, h_) for h_ in (1 - h, h) for y_ in (yo, yr, yl, y)]

    def halve(f, i):
        chunk = row_of(order[i][0], order[i][1], 1 - c)

        def body(b):
            p2_v[f, chunk * 4 + b] = partial2(f, chunk, b).astype(BF)

        each(0, 4, body)
        send(f"Es{f}{i}", part(p2_v, f, chunk), sib.at[f, i], sibling)

    def halved(f, i):
        recv(f"Es{f}{i}", sib.at[f, i], sibling)

    def chunk_of(i):
        return row_of(order[i][0], order[i][1], c)

    def both(f, i, b):
        return partial2(f, chunk_of(i), b) + sib[f, i, b].astype(F32)

    def emit(name, f, i, lo, value, to, device):
        chunk = chunk_of(i)

        def body(b):
            p2_v[f, chunk * 4 + lo + b] = value(b).astype(BF)

        each(0, 2, body)
        send(name, part(p2_v, f, chunk, lo, lo + 2), to, device)

    def relay2(f, g):
        i = 4 * g
        halved(f, i)
        emit(f"Err{f}{g}", f, i, 0, lambda b: both(f, i, b), rl2.at[f, g], up)
        emit(f"Erl{f}{g}", f, i, 2, lambda b: both(f, i, b + 2), rr2.at[f, g], down)

    def raw2(f, g):
        i = 4 * g + 1
        halved(f, i)
        emit(f"Ewr{f}{g}", f, i, 2, lambda b: both(f, i, b + 2), pair(rxl2, f, g, 2), up)
        k = 4 * g + 2
        halved(f, k)
        emit(f"Ewl{f}{g}", f, k, 0, lambda b: both(f, k, b), pair(rxr2, f, g, 0), down)

    def summed2(f, g):
        i = 4 * g + 1
        recv(f"Err{f}{g}", rl2.at[f, g], down)
        emit(
            f"Esr{f}{g}", f, i, 0, lambda b: both(f, i, b) + rl2[f, g, b].astype(F32),
            pair(rxl2, f, g, 0), up,
        )
        k = 4 * g + 2
        recv(f"Erl{f}{g}", rr2.at[f, g], up)
        emit(
            f"Esl{f}{g}", f, k, 2, lambda b: both(f, k, b + 2) + rr2[f, g, b].astype(F32),
            pair(rxr2, f, g, 2), down,
        )

    def gathered2(f, g):
        halved(f, 4 * g + 3)
        recv(f"Ewr{f}{g}", pair(rxl2, f, g, 2), down)
        recv(f"Ewl{f}{g}", pair(rxr2, f, g, 0), up)
        recv(f"Esr{f}{g}", pair(rxl2, f, g, 0), down)
        recv(f"Esl{f}{g}", pair(rxr2, f, g, 2), up)

    def total2(f, g, b):
        return both(f, 4 * g + 3, b) + rxl2[f, g, b].astype(F32) + rxr2[f, g, b].astype(F32)

    def cross(f):
        gathered2(f, 0)

        def body(b):
            zs2[f, b] = total2(f, 0, b).astype(BF)

        each(0, 4, body)
        send(f"Ez{f}", zs2.at[f], rz2.at[f], across_dev)

    for i in range(8):
        halve(0, i)
    relay2(0, 0)
    raw2(0, 0)
    for k in (1, 2, 3):
        frm = (y + 4 - k) % 4
        recv(f"Gy{k}", gy.at[frm], row_dev(frm, h, c))
    g3[...] = gy[0] + gy[1] + gy[2] + gy[3]
    send("Gc", g3, gc, sibling)
    relay2(0, 1)
    passed(1)

    quarter = spmm(1, 4, g_v, a_v)
    quarter(0)
    summed2(0, 0)
    quarter(1)
    raw2(0, 1)
    quarter(2)
    recv("Gc", gc, sibling)
    g4[...] = g3[...] + gc[...]
    send("Gh", g4, gh, across_dev)
    quarter(3)

    for i in range(3):
        halve(1, i)
    cross(0)
    relay2(1, 0)
    for i in range(3, 7):
        halve(1, i)
    raw2(1, 0)
    summed2(0, 1)
    relay2(1, 1)
    halve(1, 7)
    recv("Gh", gh, across_dev)
    at = pl.multiple_of(x * 32 + z * 8, 8)
    scale = 1.0 / math.sqrt(BLK * BLOCKS * 16)
    gwf[pl.ds(at, 8), :] = (g4[...] + gh[...]) * scale
    for k in (1, 2, 3):
        piece = gwf.at[pl.ds(at, 8)]
        send(f"Gu{k}", piece, piece, col_dev(x, (z + k) % 4))
    done = taken()
    summed2(1, 0)
    raw2(1, 1)
    gathered2(0, 1)
    cross(1)
    summed2(1, 1)
    for k in (1, 2, 3):
        frm = (z + 4 - k) % 4
        recv(f"Gu{k}", gwf.at[pl.ds(pl.multiple_of(x * 32 + frm * 8, 8), 8)], col_dev(x, frm))
    for k in (1, 2, 3):
        piece = gwf.at[pl.ds(pl.multiple_of(x * 32, 32), 32)]
        send(f"Gv{k}", piece, piece, col_dev((x + k) % 4, z))
    flush(done)
    gathered2(1, 1)
    for f in range(2):
        recv(f"Ez{f}", rz2.at[f], across_dev)

    def output(b):
        total = [total2(f, 1, b) + rz2[f, b].astype(F32) for f in range(2)]
        gi_v[b] = jnp.concatenate(total, axis=0).T.astype(BF)

    each(0, 4, output)
    store_i = pltpu.make_async_copy(gi_v, gi_out, local_sem.at[6])
    store_i.start()
    for k in (1, 2, 3):
        frm = (x + 4 - k) % 4
        recv(f"Gv{k}", gwf.at[pl.ds(pl.multiple_of(frm * 32, 32), 32)], col_dev(frm, z))
    store_w = pltpu.make_async_copy(gwf, gw_out, local_sem.at[7])
    store_w.start()
    flush(taken())
    store_a.wait()
    store_i.wait()
    store_w.wait()


def leave(act, gi, gw, act_out, gi_out, gw_out, sem):
    copies = [
        pltpu.make_async_copy(src, dst, sem.at[k])
        for k, (src, dst) in enumerate(((act, act_out), (gi, gi_out), (gw, gw_out)))
    ]
    for copy in copies:
        copy.start()
    for copy in copies:
        copy.wait()


def on_device(features, weight, cotangent, adj_blocks, block_rows, block_cols, live_mask):
    hbm = pl.BlockSpec(memory_space=pl.ANY)
    vmem = pl.BlockSpec(memory_space=pltpu.VMEM)
    quad = (4, BLK, BLK)
    half = (4, HALF, BLK)
    scratch = [
        pltpu.VMEM((SLOTS, BLK, BLK), BF),
        pltpu.VMEM((SLOTS, BLK, BLK), BF),
        pltpu.VMEM(quad, BF),
        pltpu.VMEM((BLOCKS, HALF, BLK), BF),
        pltpu.VMEM((BLOCKS, HALF, BLK), BF),
        pltpu.VMEM((2, SLOTS + 1, HALF, BLK), F32),
        pltpu.VMEM((2, BLOCKS, HALF, BLK), BF),
        pltpu.VMEM((BLOCKS, HALF, BLK), BF),
        pltpu.VMEM((BLOCKS, HALF, BLK), BF),
        pltpu.VMEM((2, BLOCKS, HALF, BLK), BF),
        pltpu.VMEM((BLK, 2 * BLK), BF),
        pltpu.VMEM((4, BLK, 2 * BLK), BF),
        pltpu.VMEM((4, BLK, 2 * BLK), BF),
        pltpu.VMEM((4, BLK, 2 * BLK), BF),
        pltpu.VMEM(quad, BF),
        pltpu.VMEM(quad, BF),
        pltpu.VMEM(quad, BF),
        pltpu.VMEM((2, 4, 2, HALF, BLK), BF),
        pltpu.VMEM((2, 4, 2, HALF, BLK), BF),
        pltpu.VMEM((2, 4) + half, BF),
        pltpu.VMEM((2, 4) + half, BF),
        pltpu.VMEM((2, 3) + half, BF),
        pltpu.VMEM((2, 3) + half, BF),
        pltpu.VMEM((2,) + half, F32),
        pltpu.VMEM((2, 8) + half, BF),
        pltpu.VMEM((2, 2, 2, HALF, BLK), BF),
        pltpu.VMEM((2, 2, 2, HALF, BLK), BF),
        pltpu.VMEM((2, 2) + half, BF),
        pltpu.VMEM((2, 2) + half, BF),
        pltpu.VMEM((2,) + half, BF),
        pltpu.VMEM((2,) + half, BF),
        pltpu.VMEM((BLK, 2 * BLK), F32),
        pltpu.VMEM((3, 32, 2 * BLK), F32),
        pltpu.VMEM((32, 2 * BLK), F32),
        pltpu.VMEM((3, 8, 2 * BLK), F32),
        pltpu.VMEM((4, 8, 2 * BLK), F32),
        pltpu.VMEM((8, 2 * BLK), F32),
        pltpu.VMEM((8, 2 * BLK), F32),
        pltpu.VMEM((8, 2 * BLK), F32),
        pltpu.VMEM((8, 2 * BLK), F32),
        pltpu.VMEM((BLK, 2 * BLK), F32),
        pltpu.VMEM((8, SLOTS), jnp.int32),
        pltpu.SMEM((8, SLOTS), jnp.int32),
        pltpu.SemaphoreType.DMA((192,)),
        pltpu.SemaphoreType.DMA((192,)),
        pltpu.SemaphoreType.DMA((8,)),
    ]
    outs = (
        jax.ShapeDtypeStruct((4, BLK, 2 * BLK), BF),
        jax.ShapeDtypeStruct(quad, BF),
        jax.ShapeDtypeStruct((BLK, 2 * BLK), F32),
    )
    held = pl.pallas_call(
        kernel,
        out_shape=outs,
        in_specs=[hbm, hbm, hbm, hbm, vmem, vmem, vmem],
        out_specs=(hbm, hbm, hbm),
        scratch_shapes=scratch,
        compiler_params=pltpu.CompilerParams(
            collective_id=0, has_side_effects=True, vmem_limit_bytes=60 << 20
        ),
        cost_estimate=pl.CostEstimate(flops=2 << 30, bytes_accessed=12 << 20, transcendentals=1 << 17),
        name="graph_layer",
    )(
        features.reshape(quad),
        weight,
        cotangent.reshape(4, BLK, 2 * BLK),
        adj_blocks.reshape(SLOTS, BLK, BLK),
        block_rows.reshape(1, SLOTS),
        block_cols.reshape(1, SLOTS),
        live_mask.reshape(1, SLOTS),
    )
    act, gi, gw = pl.pallas_call(
        leave,
        out_shape=outs,
        in_specs=[hbm] * 3,
        out_specs=(vmem,) * 3,
        scratch_shapes=[pltpu.SemaphoreType.DMA((3,))],
        name="leave",
    )(*held)
    return act.reshape(4 * BLK, 2 * BLK), gi.reshape(4 * BLK, BLK), gw


def solution(mesh):
    in_specs = (
        P(("col", "row"), None),
        P(),
        P(("row", "col"), None),
        P("row", "col", None, None, None),
        P("row", "col", None),
        P("row", "col", None),
        P("row", "col", None),
    )
    out_specs = (P(("row", "col"), None), P(("col", "row"), None), P())
    return jax.shard_map(
        on_device, mesh=mesh, in_specs=in_specs, out_specs=out_specs, check_vma=False
    )
```

```python
import functools
import math

import jax
import jax.numpy as jnp
from jax import lax
from jax.experimental import pallas as pl
from jax.experimental.pallas import tpu as pltpu
from jax.sharding import PartitionSpec as P

MESH = pl.DeviceIdType.MESH
BF = jnp.bfloat16
F32 = jnp.float32
BLK = 128
SLOTS = 256
BLOCKS = 64
HALF = 64
STRAIGHT = ((0, 3), (1, 2), (1, 3))
UNROLL = 64


def slot_tables(put, pick, live):
    shape = (SLOTS, SLOTS)
    put_lane = jnp.broadcast_to(jnp.where(live != 0, put, BLOCKS), shape)
    put_sub = put_lane.T
    pick_sub = jnp.broadcast_to(pick, shape).T
    sub = lax.broadcasted_iota(jnp.int32, shape, 0)
    lane = lax.broadcasted_iota(jnp.int32, shape, 1)

    def count(mask, axis):
        return jnp.sum(mask.astype(jnp.int32), axis=axis, keepdims=True)

    rank = count(put_lane * SLOTS + lane < put_sub * SLOTS + sub, 1)
    chosen = rank == lane
    continues = count((put_lane == put_sub) & (lane < sub), 1) > 0
    order = jnp.sum(jnp.where(chosen, sub, 0), axis=0, keepdims=True)
    source = jnp.sum(jnp.where(chosen, pick_sub, 0), axis=0, keepdims=True)
    follow = count(chosen & continues, 0)
    held = count(put_sub == lane, 0)
    upto = count(put_sub <= lane, 0)
    last = jnp.where(held > 0, upto - 1, SLOTS)
    return order, source, follow, last


def kernel(
    feat, weight, cot, adj, rows, cols, live,
    act_out, gi_out, gw_out,
    a_v, at_v, f_v, x_0, x_1, s_v, p_v, g_0, g_1, p2_v, w_v, cot_v, act_v, gp_v, hi_v, lo_v, gi_v,
    rl, rr, rxl, rxr, zs, rz, tz,
    sib, ro2, rl2, rr2, rxl2, rxr2, zs2, rz2,
    gwp, gx, g1, gz, gy, g3, gc, g4, gh, gwf,
    tab_v, tab, send_sem, recv_sem, local_sem,
):
    row = lax.axis_index("row")
    col = lax.axis_index("col")
    y, h, c = row // 4, (row // 2) % 2, row % 2
    x, z = col // 4, col % 4
    xr, xo, xl = (x + 1) % 4, (x + 2) % 4, (x + 3) % 4
    yr, yo, yl = (y + 1) % 4, (y + 2) % 4, (y + 3) % 4

    def col_dev(x_, z_):
        return (row, x_ * 4 + z_)

    def row_of(y_, h_, c_):
        return y_ * 4 + h_ * 2 + c_

    def row_dev(y_, h_, c_):
        return (row_of(y_, h_, c_), col)

    x_v, g_v = (x_0, x_1), (g_0, g_1)
    to_r, to_l, to_o = col_dev(xr, z), col_dev(xl, z), col_dev(xo, z)
    up, down, over = row_dev(yr, h, c), row_dev(yl, h, c), row_dev(yo, h, c)
    across_dev, sibling = row_dev(y, 1 - h, c), row_dev(y, h, 1 - c)

    peers = [to_r, col_dev(xo, z), to_l]
    peers += [col_dev(x, (z + d) % 4) for d in (1, 2, 3)]
    peers += [up, over, down, across_dev, sibling]
    barrier = pltpu.get_barrier_semaphore()
    for peer in peers:
        pl.semaphore_signal(barrier, inc=1, device_id=peer, device_id_type=MESH)

    names = {}
    pending = []

    def number(name):
        return names.setdefault(name, len(names))

    def send(name, src, dst, device):
        k = number(name)
        copy = pltpu.make_async_remote_copy(
            src_ref=src, dst_ref=dst, send_sem=send_sem.at[k], recv_sem=recv_sem.at[k],
            device_id=device, device_id_type=MESH,
        )
        copy.start()
        pending.append(copy)

    def recv(name, dst, device):
        k = number(name)
        pltpu.make_async_remote_copy(
            src_ref=dst, dst_ref=dst, send_sem=send_sem.at[k], recv_sem=recv_sem.at[k],
            device_id=device, device_id_type=MESH,
        ).wait_recv()

    def flush(copies):
        for copy in copies:
            copy.wait_send()

    def taken():
        copies = list(pending)
        del pending[:]
        return copies

    def each(lo, hi, body):
        def step(b, carry):
            body(b)
            return carry

        lax.fori_loop(lo, hi, step, 0, unroll=hi - lo)

    load_f = pltpu.make_async_copy(feat, f_v, local_sem.at[3])
    load_f.start()
    load_a = pltpu.make_async_copy(adj, a_v, local_sem.at[0])
    load_a.start()
    load_w = pltpu.make_async_copy(weight, w_v, local_sem.at[1])
    load_w.start()
    load_c = pltpu.make_async_copy(cot, cot_v, local_sem.at[2])
    load_c.start()

    def part(ref, f, chunk, lo=0, hi=4):
        at = pl.ds(chunk * 4 + lo, hi - lo)
        return ref[f].at[at] if isinstance(ref, tuple) else ref.at[f, at]

    load_f.wait()

    def turn(b):
        turned = f_v[b].T
        x_0[row * 4 + b] = turned[:HALF]
        x_1[row * 4 + b] = turned[HALF:]

    each(0, 4, turn)
    pl.semaphore_wait(barrier, len(peers))

    def begin(f):
        own = part(x_v, f, row)
        send(f"Az{f}", own, own, across_dev)
        send(f"Ar{f}", own, own, up)
        send(f"Al{f}", own, own, down)
        send(f"As{f}", own, own, sibling)

    begin(0)
    table = slot_tables(rows[...], cols[...], live[...])
    for k in range(4):
        tab_v[k : k + 1, :] = table[k]
    table = slot_tables(cols[...], rows[...], live[...])
    for k in range(4):
        tab_v[k + 4 : k + 5, :] = table[k]
    load_t = pltpu.make_async_copy(tab_v, tab, local_sem.at[4])
    load_t.start()
    for f in range(2):
        s_v[f, SLOTS] = jnp.zeros((HALF, BLK), F32)

    def share(name, f, chunk, lo=0, hi=4):
        send("S" + name, part(x_v, f, chunk, lo, hi), part(x_v, f, chunk, lo, hi), sibling)

    left, right, opp = row_of(yl, h, c), row_of(yr, h, c), row_of(yo, h, c)
    across = row_of(y, 1 - h, c)
    far = [row_of(yl, 1 - h, c), row_of(yr, 1 - h, c), row_of(yo, 1 - h, c)]

    def beside(f):
        recv(f"Ar{f}", part(x_v, f, left), down)
        send(f"Arr{f}", part(x_v, f, left, 0, 2), part(x_v, f, left, 0, 2), up)
        share(f"l{f}", f, left)
        recv(f"Al{f}", part(x_v, f, right), up)
        send(f"All{f}", part(x_v, f, right, 2, 4), part(x_v, f, right, 2, 4), down)
        share(f"r{f}", f, right)

    def crossed(f):
        piece = part(x_v, f, across)
        recv(f"Az{f}", piece, across_dev)
        send(f"Afr{f}", piece, piece, up)
        send(f"Afl{f}", piece, piece, down)
        send(f"Afo{f}", piece, piece, over)
        share(f"z{f}", f, across)

    def opposite(f):
        recv(f"Arr{f}", part(x_v, f, opp, 0, 2), down)
        share(f"oa{f}", f, opp, 0, 2)
        recv(f"All{f}", part(x_v, f, opp, 2, 4), up)
        share(f"ob{f}", f, opp, 2, 4)

    def remote(f):
        recv(f"Afr{f}", part(x_v, f, far[0]), down)
        share(f"fl{f}", f, far[0])
        recv(f"Afl{f}", part(x_v, f, far[1]), up)
        share(f"fr{f}", f, far[1])
        recv(f"Afo{f}", part(x_v, f, far[2]), over)
        share(f"fo{f}", f, far[2])

    def shared(f):
        d = 1 - c

        def take(name, chunk, lo=0, hi=4):
            recv(name, part(x_v, f, chunk, lo, hi), sibling)

        take(f"As{f}", row_of(y, h, d))
        take(f"Sl{f}", row_of(yl, h, d))
        take(f"Sr{f}", row_of(yr, h, d))
        take(f"Sz{f}", row_of(y, 1 - h, d))
        take(f"Soa{f}", row_of(yo, h, d), 0, 2)
        take(f"Sob{f}", row_of(yo, h, d), 2, 4)
        take(f"Sfl{f}", row_of(yl, 1 - h, d))
        take(f"Sfr{f}", row_of(yr, 1 - h, d))
        take(f"Sfo{f}", row_of(yo, 1 - h, d))

    def turn_blocks(n):
        def step(k, carry):
            at_v[k] = a_v[k].T
            return carry

        lax.fori_loop(64 * n, 64 * n + 64, step, 0, unroll=16)

    def spmm(f, base, source, blocks):
        def step(k, total):
            block = blocks[tab[base, k]]
            other = source[f][tab[base + 1, k]]
            product = jnp.dot(other, block, preferred_element_type=F32)
            total = jnp.where(tab[base + 2, k] != 0, total, 0.0) + product
            s_v[f, k] = total
            return total

        held = [jnp.zeros((HALF, BLK), F32)]

        def quarter(n):
            held[0] = lax.fori_loop(64 * n, 64 * n + 64, step, held[0], unroll=64)

        return quarter

    beside(0)
    begin(1)
    crossed(0)
    load_a.wait()
    turn_blocks(0)
    opposite(0)
    beside(1)
    turn_blocks(1)
    crossed(1)
    turn_blocks(2)
    remote(0)
    turn_blocks(3)
    opposite(1)
    load_t.wait()
    shared(0)
    quarter = spmm(0, 0, x_v, at_v)
    for n in range(4):
        quarter(n)

    def partial(f, chunk, b):
        return s_v[f, tab[3, chunk * 4 + b]]

    def fill(f, chunk, lo, hi):
        def body(b):
            p_v[f, chunk * 4 + b] = partial(f, chunk, b).astype(BF)

        each(lo, hi, body)

    zj = [(z + 1 + j) % 4 for j in range(4)]

    def pair(ref, f, j, lo):
        return ref.at[f, j, pl.ds(lo, 2)]

    def relay(f, j):
        chunk = xo * 4 + zj[j]
        fill(f, chunk, 0, 4)
        send(f"Brr{f}{j}", part(p_v, f, chunk, 0, 2), rl.at[f, j], to_r)
        send(f"Brl{f}{j}", part(p_v, f, chunk, 2, 4), rr.at[f, j], to_l)

    def raw(f, j):
        chunk = xr * 4 + zj[j]
        fill(f, chunk, 2, 4)
        send(f"Bwr{f}{j}", part(p_v, f, chunk, 2, 4), pair(rxl, f, j, 2), to_r)
        chunk = xl * 4 + zj[j]
        fill(f, chunk, 0, 2)
        send(f"Bwl{f}{j}", part(p_v, f, chunk, 0, 2), pair(rxr, f, j, 0), to_l)

    def summed(f, j):
        chunk_r = xr * 4 + zj[j]
        recv(f"Brr{f}{j}", rl.at[f, j], to_l)

        def body_r(b):
            p_v[f, chunk_r * 4 + b] = (partial(f, chunk_r, b) + rl[f, j, b].astype(F32)).astype(BF)

        each(0, 2, body_r)
        send(f"Bsr{f}{j}", part(p_v, f, chunk_r, 0, 2), pair(rxl, f, j, 0), to_r)
        chunk_l = xl * 4 + zj[j]
        recv(f"Brl{f}{j}", rr.at[f, j], to_r)

        def body_l(b):
            p_v[f, chunk_l * 4 + 2 + b] = (
                partial(f, chunk_l, b + 2) + rr[f, j, b].astype(F32)
            ).astype(BF)

        each(0, 2, body_l)
        send(f"Bsl{f}{j}", part(p_v, f, chunk_l, 2, 4), pair(rxr, f, j, 2), to_l)

    def finish(f, j):
        recv(f"Bwr{f}{j}", pair(rxl, f, j, 2), to_l)
        recv(f"Bwl{f}{j}", pair(rxr, f, j, 0), to_r)
        recv(f"Bsr{f}{j}", pair(rxl, f, j, 0), to_l)
        recv(f"Bsl{f}{j}", pair(rxr, f, j, 2), to_r)
        chunk = x * 4 + zj[j]

        def body(b):
            total = partial(f, chunk, b) + rxl[f, j, b].astype(F32) + rxr[f, j, b].astype(F32)
            if j < 3:
                zs[f, j, b] = total.astype(BF)
            else:
                tz[f, b] = total

        each(0, 4, body)
        if j < 3:
            send(f"Bz{f}{j}", zs.at[f, j], rz.at[f, j], col_dev(x, zj[j]))

    quarter = spmm(1, 0, x_v, at_v)
    relay(0, 0)
    raw(0, 0)
    relay(0, 1)
    remote(1)
    summed(0, 0)
    raw(0, 1)
    relay(0, 2)
    shared(1)
    quarter(0)
    summed(0, 1)
    raw(0, 2)
    relay(0, 3)
    quarter(1)
    finish(0, 0)
    raw(0, 3)
    quarter(2)
    summed(0, 2)
    finish(0, 1)
    quarter(3)
    relay(1, 0)
    summed(0, 3)
    raw(1, 0)
    relay(1, 1)
    finish(0, 2)
    done = taken()
    summed(1, 0)
    raw(1, 1)
    relay(1, 2)
    finish(0, 3)
    summed(1, 1)
    raw(1, 2)
    relay(1, 3)
    finish(1, 0)
    summed(1, 2)
    raw(1, 3)
    finish(1, 1)
    summed(1, 3)
    flush(done)
    finish(1, 2)
    load_w.wait()
    load_c.wait()
    finish(1, 3)
    for f in range(2):
        for j in range(3):
            recv(f"Bz{f}{j}", rz.at[f, j], col_dev(x, (z + 3 - j) % 4))

    def layer(b):
        agg = jnp.concatenate(
            [
                tz[f, b] + rz[f, 0, b].astype(F32) + rz[f, 1, b].astype(F32) + rz[f, 2, b].astype(F32)
                for f in range(2)
            ],
            axis=0,
        ).T
        high = agg.astype(BF)
        low = (agg - high.astype(F32)).astype(BF)
        hi_v[b] = high
        lo_v[b] = low
        w = w_v[...]
        pre = jnp.dot(high, w, preferred_element_type=F32) + jnp.dot(low, w, preferred_element_type=F32)
        s = lax.logistic(pre)
        act_v[b] = (pre * s).astype(BF)
        grad = (cot_v[b].astype(F32) * s * (1.0 + pre * (1.0 - s))).astype(BF)
        gp_v[b] = grad
        narrow = lax.dot_general(w, grad, (((1,), (1,)), ((), ())), preferred_element_type=F32)
        narrow = narrow.astype(BF)
        g_0[col * 4 + b] = narrow[:HALF]
        g_1[col * 4 + b] = narrow[HALF:]

    each(0, 4, layer)

    zsrc = [z, (z + 3) % 4, (z + 1) % 4, (z + 2) % 4]
    zdst = [z, (z + 1) % 4, (z + 3) % 4, (z + 2) % 4]

    def along(f, s):
        chunk = part(g_v, f, x * 4 + zsrc[s])
        if s > 0:
            recv(f"Cz{f}{s}", chunk, col_dev(x, zsrc[s]))
        send(f"Cr{f}{s}", chunk, chunk, to_r)
        send(f"Cl{f}{s}", chunk, chunk, to_l)
        if (f, s) in STRAIGHT:
            send(f"Co{f}{s}", chunk, chunk, to_o)

    def pass_on(f, s):
        chunk = xl * 4 + zsrc[s]
        recv(f"Cr{f}{s}", part(g_v, f, chunk), to_l)
        if (f, s) not in STRAIGHT:
            send(f"Crr{f}{s}", part(g_v, f, chunk, 0, 2), part(g_v, f, chunk, 0, 2), to_r)
        chunk = xr * 4 + zsrc[s]
        recv(f"Cl{f}{s}", part(g_v, f, chunk), to_r)
        if (f, s) not in STRAIGHT:
            send(f"Cll{f}{s}", part(g_v, f, chunk, 2, 4), part(g_v, f, chunk, 2, 4), to_l)

    def passed(f):
        for s in range(4):
            chunk = xo * 4 + zsrc[s]
            if (f, s) in STRAIGHT:
                recv(f"Co{f}{s}", part(g_v, f, chunk), to_o)
            else:
                recv(f"Crr{f}{s}", part(g_v, f, chunk, 0, 2), to_l)
                recv(f"Cll{f}{s}", part(g_v, f, chunk, 2, 4), to_r)

    def beyond(f, s):
        mine = part(g_v, f, col)
        send(f"Cz{f}{s}", mine, mine, col_dev(x, zdst[s]))

    along(0, 0)
    beyond(0, 1)
    beyond(0, 2)
    along(1, 0)
    store_a = pltpu.make_async_copy(act_v, act_out, local_sem.at[5])
    store_a.start()

    gwp[...] = jnp.zeros_like(gwp)

    def weight_term(b):
        dims = (((0,), (0,)), ((), ()))
        grad = gp_v[b]
        gwp[...] += lax.dot_general(hi_v[b], grad, dims, preferred_element_type=F32) + lax.dot_general(
            lo_v[b], grad, dims, preferred_element_type=F32
        )

    each(0, 4, weight_term)
    for k in (1, 2, 3):
        to = (x + k) % 4
        send(f"Gx{k}", gwp.at[pl.ds(pl.multiple_of(to * 32, 32), 32)], gx.at[k - 1], col_dev(to, z))

    along(0, 1)
    beyond(0, 3)
    along(0, 2)
    beyond(1, 1)
    beyond(1, 2)
    pass_on(0, 0)
    for k in (1, 2, 3):
        recv(f"Gx{k}", gx.at[k - 1], col_dev((x + 4 - k) % 4, z))
    g1[...] = gwp[pl.ds(pl.multiple_of(x * 32, 32), 32), :] + gx[0] + gx[1] + gx[2]
    for k in (1, 2, 3):
        to = (z + k) % 4
        send(f"Gz{k}", g1.at[pl.ds(pl.multiple_of(to * 8, 8), 8)], gz.at[k - 1], col_dev(x, to))
    along(0, 3)
    pass_on(0, 1)
    along(1, 1)
    beyond(1, 3)
    pass_on(0, 2)
    along(1, 2)
    pass_on(1, 0)
    for k in (1, 2, 3):
        recv(f"Gz{k}", gz.at[k - 1], col_dev(x, (z + 4 - k) % 4))
    gy[y] = g1[pl.ds(pl.multiple_of(z * 8, 8), 8), :] + gz[0] + gz[1] + gz[2]
    for k in (1, 2, 3):
        send(f"Gy{k}", gy.at[y], gy.at[y], row_dev((y + k) % 4, h, c))
    pass_on(0, 3)
    along(1, 3)
    passed(0)

    quarter = spmm(0, 4, g_v, a_v)
    quarter(0)
    pass_on(1, 1)
    quarter(1)
    pass_on(1, 2)
    quarter(2)
    quarter(3)
    pass_on(1, 3)

    def partial2(f, chunk, b):
        return s_v[f, tab[7, chunk * 4 + b]]

    order = [(y_, h_) for h_ in (1 - h, h) for y_ in (yo, yr, yl, y)]

    def halve(f, i):
        chunk = row_of(order[i][0], order[i][1], 1 - c)

        def body(b):
            p2_v[f, chunk * 4 + b] = partial2(f, chunk, b).astype(BF)

        each(0, 4, body)
        send(f"Es{f}{i}", part(p2_v, f, chunk), sib.at[f, i], sibling)

    def halved(f, i):
        recv(f"Es{f}{i}", sib.at[f, i], sibling)

    def chunk_of(i):
        return row_of(order[i][0], order[i][1], c)

    def both(f, i, b):
        return partial2(f, chunk_of(i), b) + sib[f, i, b].astype(F32)

    def emit(name, f, i, lo, value, to, device, n=2):
        chunk = chunk_of(i)

        def body(b):
            p2_v[f, chunk * 4 + lo + b] = value(b).astype(BF)

        each(0, n, body)
        send(name, part(p2_v, f, chunk, lo, lo + n), to, device)

    def relay2(f, g):
        i = 4 * g
        halved(f, i)
        if g == 0:
            emit(f"Ewo{f}", f, i, 0, lambda b: both(f, i, b), ro2.at[f], over, 4)
            return
        emit(f"Err{f}{g}", f, i, 0, lambda b: both(f, i, b), rl2.at[f, g], up)
        emit(f"Erl{f}{g}", f, i, 2, lambda b: both(f, i, b + 2), rr2.at[f, g], down)

    def raw2(f, g):
        i = 4 * g + 1
        halved(f, i)
        if g == 0:
            emit(f"Ewr{f}0", f, i, 0, lambda b: both(f, i, b), rxl2.at[f, 0], up, 4)
            halved(f, i + 1)
            emit(f"Ewl{f}0", f, i + 1, 0, lambda b: both(f, i + 1, b), rxr2.at[f, 0], down, 4)
            return
        emit(f"Ewr{f}{g}", f, i, 2, lambda b: both(f, i, b + 2), pair(rxl2, f, g, 2), up)
        k = 4 * g + 2
        halved(f, k)
        emit(f"Ewl{f}{g}", f, k, 0, lambda b: both(f, k, b), pair(rxr2, f, g, 0), down)

    def summed2(f, g):
        if g == 0:
            return
        i = 4 * g + 1
        recv(f"Err{f}{g}", rl2.at[f, g], down)
        emit(
            f"Esr{f}{g}", f, i, 0, lambda b: both(f, i, b) + rl2[f, g, b].astype(F32),
            pair(rxl2, f, g, 0), up,
        )
        k = 4 * g + 2
        recv(f"Erl{f}{g}", rr2.at[f, g], up)
        emit(
            f"Esl{f}{g}", f, k, 2, lambda b: both(f, k, b + 2) + rr2[f, g, b].astype(F32),
            pair(rxr2, f, g, 2), down,
        )

    def gathered2(f, g):
        halved(f, 4 * g + 3)
        if g == 0:
            recv(f"Ewr{f}0", rxl2.at[f, 0], down)
            recv(f"Ewl{f}0", rxr2.at[f, 0], up)
            recv(f"Ewo{f}", ro2.at[f], over)
            return
        recv(f"Ewr{f}{g}", pair(rxl2, f, g, 2), down)
        recv(f"Ewl{f}{g}", pair(rxr2, f, g, 0), up)
        recv(f"Esr{f}{g}", pair(rxl2, f, g, 0), down)
        recv(f"Esl{f}{g}", pair(rxr2, f, g, 2), up)

    def total2(f, g, b):
        return both(f, 4 * g + 3, b) + rxl2[f, g, b].astype(F32) + rxr2[f, g, b].astype(F32)

    def cross(f):
        gathered2(f, 0)

        def body(b):
            zs2[f, b] = (total2(f, 0, b) + ro2[f, b].astype(F32)).astype(BF)

        each(0, 4, body)
        send(f"Ez{f}", zs2.at[f], rz2.at[f], across_dev)

    for i in range(8):
        halve(0, i)
    relay2(0, 0)
    raw2(0, 0)
    for k in (1, 2, 3):
        frm = (y + 4 - k) % 4
        recv(f"Gy{k}", gy.at[frm], row_dev(frm, h, c))
    g3[...] = gy[0] + gy[1] + gy[2] + gy[3]
    send("Gc", g3, gc, sibling)
    relay2(0, 1)
    passed(1)

    quarter = spmm(1, 4, g_v, a_v)
    quarter(0)
    summed2(0, 0)
    quarter(1)
    raw2(0, 1)
    quarter(2)
    recv("Gc", gc, sibling)
    g4[...] = g3[...] + gc[...]
    send("Gh", g4, gh, across_dev)
    quarter(3)

    for i in range(3):
        halve(1, i)
    cross(0)
    relay2(1, 0)
    for i in range(3, 7):
        halve(1, i)
    raw2(1, 0)
    summed2(0, 1)
    relay2(1, 1)
    halve(1, 7)
    recv("Gh", gh, across_dev)
    at = pl.multiple_of(x * 32 + z * 8, 8)
    scale = 1.0 / math.sqrt(BLK * BLOCKS * 16)
    gwf[pl.ds(at, 8), :] = (g4[...] + gh[...]) * scale
    for k in (1, 2, 3):
        piece = gwf.at[pl.ds(at, 8)]
        send(f"Gu{k}", piece, piece, col_dev(x, (z + k) % 4))
    done = taken()
    summed2(1, 0)
    raw2(1, 1)
    gathered2(0, 1)
    cross(1)
    summed2(1, 1)
    for k in (1, 2, 3):
        frm = (z + 4 - k) % 4
        recv(f"Gu{k}", gwf.at[pl.ds(pl.multiple_of(x * 32 + frm * 8, 8), 8)], col_dev(x, frm))
    for k in (1, 2, 3):
        piece = gwf.at[pl.ds(pl.multiple_of(x * 32, 32), 32)]
        send(f"Gv{k}", piece, piece, col_dev((x + k) % 4, z))
    flush(done)
    gathered2(1, 1)
    for f in range(2):
        recv(f"Ez{f}", rz2.at[f], across_dev)

    def output(b):
        total = [total2(f, 1, b) + rz2[f, b].astype(F32) for f in range(2)]
        gi_v[b] = jnp.concatenate(total, axis=0).T.astype(BF)

    each(0, 4, output)
    store_i = pltpu.make_async_copy(gi_v, gi_out, local_sem.at[6])
    store_i.start()
    for k in (1, 2, 3):
        frm = (x + 4 - k) % 4
        recv(f"Gv{k}", gwf.at[pl.ds(pl.multiple_of(frm * 32, 32), 32)], col_dev(frm, z))
    store_w = pltpu.make_async_copy(gwf, gw_out, local_sem.at[7])
    store_w.start()
    flush(taken())
    store_a.wait()
    store_i.wait()
    store_w.wait()


def leave(act, gi, gw, act_out, gi_out, gw_out, sem):
    copies = [
        pltpu.make_async_copy(src, dst, sem.at[k])
        for k, (src, dst) in enumerate(((act, act_out), (gi, gi_out), (gw, gw_out)))
    ]
    for copy in copies:
        copy.start()
    for copy in copies:
        copy.wait()


def on_device(features, weight, cotangent, adj_blocks, block_rows, block_cols, live_mask):
    hbm = pl.BlockSpec(memory_space=pl.ANY)
    vmem = pl.BlockSpec(memory_space=pltpu.VMEM)
    quad = (4, BLK, BLK)
    half = (4, HALF, BLK)
    scratch = [
        pltpu.VMEM((SLOTS, BLK, BLK), BF),
        pltpu.VMEM((SLOTS, BLK, BLK), BF),
        pltpu.VMEM(quad, BF),
        pltpu.VMEM((BLOCKS, HALF, BLK), BF),
        pltpu.VMEM((BLOCKS, HALF, BLK), BF),
        pltpu.VMEM((2, SLOTS + 1, HALF, BLK), F32),
        pltpu.VMEM((2, BLOCKS, HALF, BLK), BF),
        pltpu.VMEM((BLOCKS, HALF, BLK), BF),
        pltpu.VMEM((BLOCKS, HALF, BLK), BF),
        pltpu.VMEM((2, BLOCKS, HALF, BLK), BF),
        pltpu.VMEM((BLK, 2 * BLK), BF),
        pltpu.VMEM((4, BLK, 2 * BLK), BF),
        pltpu.VMEM((4, BLK, 2 * BLK), BF),
        pltpu.VMEM((4, BLK, 2 * BLK), BF),
        pltpu.VMEM(quad, BF),
        pltpu.VMEM(quad, BF),
        pltpu.VMEM(quad, BF),
        pltpu.VMEM((2, 4, 2, HALF, BLK), BF),
        pltpu.VMEM((2, 4, 2, HALF, BLK), BF),
        pltpu.VMEM((2, 4) + half, BF),
        pltpu.VMEM((2, 4) + half, BF),
        pltpu.VMEM((2, 3) + half, BF),
        pltpu.VMEM((2, 3) + half, BF),
        pltpu.VMEM((2,) + half, F32),
        pltpu.VMEM((2, 8) + half, BF),
        pltpu.VMEM((2,) + half, BF),
        pltpu.VMEM((2, 2, 2, HALF, BLK), BF),
        pltpu.VMEM((2, 2, 2, HALF, BLK), BF),
        pltpu.VMEM((2, 2) + half, BF),
        pltpu.VMEM((2, 2) + half, BF),
        pltpu.VMEM((2,) + half, BF),
        pltpu.VMEM((2,) + half, BF),
        pltpu.VMEM((BLK, 2 * BLK), F32),
        pltpu.VMEM((3, 32, 2 * BLK), F32),
        pltpu.VMEM((32, 2 * BLK), F32),
        pltpu.VMEM((3, 8, 2 * BLK), F32),
        pltpu.VMEM((4, 8, 2 * BLK), F32),
        pltpu.VMEM((8, 2 * BLK), F32),
        pltpu.VMEM((8, 2 * BLK), F32),
        pltpu.VMEM((8, 2 * BLK), F32),
        pltpu.VMEM((8, 2 * BLK), F32),
        pltpu.VMEM((BLK, 2 * BLK), F32),
        pltpu.VMEM((8, SLOTS), jnp.int32),
        pltpu.SMEM((8, SLOTS), jnp.int32),
        pltpu.SemaphoreType.DMA((192,)),
        pltpu.SemaphoreType.DMA((192,)),
        pltpu.SemaphoreType.DMA((8,)),
    ]
    outs = (
        jax.ShapeDtypeStruct((4, BLK, 2 * BLK), BF),
        jax.ShapeDtypeStruct(quad, BF),
        jax.ShapeDtypeStruct((BLK, 2 * BLK), F32),
    )
    held = pl.pallas_call(
        kernel,
        out_shape=outs,
        in_specs=[hbm, hbm, hbm, hbm, vmem, vmem, vmem],
        out_specs=(hbm, hbm, hbm),
        scratch_shapes=scratch,
        compiler_params=pltpu.CompilerParams(
            collective_id=0, has_side_effects=True, vmem_limit_bytes=60 << 20
        ),
        cost_estimate=pl.CostEstimate(flops=2 << 30, bytes_accessed=12 << 20, transcendentals=1 << 17),
        name="graph_layer",
    )(
        features.reshape(quad),
        weight,
        cotangent.reshape(4, BLK, 2 * BLK),
        adj_blocks.reshape(SLOTS, BLK, BLK),
        block_rows.reshape(1, SLOTS),
        block_cols.reshape(1, SLOTS),
        live_mask.reshape(1, SLOTS),
    )
    act, gi, gw = pl.pallas_call(
        leave,
        out_shape=outs,
        in_specs=[hbm] * 3,
        out_specs=(vmem,) * 3,
        scratch_shapes=[pltpu.SemaphoreType.DMA((3,))],
        name="leave",
    )(*held)
    return act.reshape(4 * BLK, 2 * BLK), gi.reshape(4 * BLK, BLK), gw


def solution(mesh):
    in_specs = (
        P(("col", "row"), None),
        P(),
        P(("row", "col"), None),
        P("row", "col", None, None, None),
        P("row", "col", None),
        P("row", "col", None),
        P("row", "col", None),
    )
    out_specs = (P(("row", "col"), None), P(("col", "row"), None), P())
    return jax.shard_map(
        on_device, mesh=mesh, in_specs=in_specs, out_specs=out_specs, check_vma=False
    )
```
